32 devices in a mesh: sa: 4 (over z), sb: 4 (over x, core), rep: 2 (over y).
Axes of the slice: x: 2, y: 2, z: 4, core: 2. Of those that a mesh axis runs over, the one named last changes fastest.
Arguments:
- queries: bfloat16 [2, 64, 64, 12288], P('rep', ('sa', 'sb')), may hold values from -90.93267 to 90.93267
- grad_out: bfloat16 [2, 64, 64, 8192], P('rep', ('sa', 'sb')), may hold values from -6 to 6
- cache_codes: bfloat16 [2, 320, 16, 576], P('rep', ('sa', 'sb')), may hold values from -4.1 to 4.1
- cache_exponents: int32 [2, 320, 16, 4], P('rep', ('sa', 'sb')), may hold values from -1 to 1
- page_table: int32 [2, 64, 5], P('rep'), may hold values from 0 to 319, as said below
- offsets: int32 [2, 64], P('rep'), may hold values from 8 to 16, as said below
- key_up: bfloat16 [64, 512, 128], P(('sa', 'sb')), may hold values from -0.25 to 0.25
- value_up: bfloat16 [64, 512, 128], P(('sa', 'sb')), may hold values from -0.25 to 0.25
Outputs:
- grad_queries: bfloat16 [2, 64, 64, 12288], P('rep', ('sa', 'sb'))
- grad_cache: float32 [2, 320, 16, 576], P('rep', ('sa', 'sb'))
- grad_key_up: float32 [64, 512, 128], P(('sa', 'sb'))
- grad_value_up: float32 [64, 512, 128], P(('sa', 'sb'))
The draws below stay inside these ranges and needn't reach their ends.
Inputs may be any that keep to these rules, and one draw needn't show every extreme that they name: `page_table`: the rows of the sequences of one replica together name each of that replica's 320 pool pages exactly once. Query i of sequence s of replica r stands at key position offsets[r, s] + i.
All inputs are finite; a program needn't handle non-finite values.
Results may differ from the reference program's by a relative error of at most 0.015.
Values may be sent and summed in bfloat16 or wider, within the bound.
A program may use at most 128 MiB of HBM per device.

```python
import jax
import jax.numpy as jnp
from jax import lax

H = 64
RANK = 512
ROPE = 64
NOPE = 128
VDIM = 128
SCALES = 4
PAGE = 16
SEQ_REP = 64
Q = 64
PREFIX = 16
CTX = 80
PAGES_REP = 320
REPLICAS = 2


def shuffle_pages(single_key):
    return jax.random.permutation(single_key, PAGES_REP)


def layout(key):
    base_key = jax.random.fold_in(key, 7001)
    total_seqs = REPLICAS * SEQ_REP
    page_keys = jax.random.split(jax.random.fold_in(base_key, 1), REPLICAS)
    pages_map = jax.vmap(shuffle_pages)(page_keys).reshape(REPLICAS, SEQ_REP, CTX // PAGE).astype(jnp.int32)
    starts = jax.random.randint(jax.random.fold_in(base_key, 2), (total_seqs,), PREFIX // 2, PREFIX + 1)
    chosen = jax.random.permutation(jax.random.fold_in(base_key, 3), total_seqs)
    starts = starts.at[chosen[0]].set(PREFIX).at[chosen[1]].set(PREFIX // 2)
    return (pages_map, starts.reshape(REPLICAS, SEQ_REP).astype(jnp.int32))


def pool_values(key):
    full_shape = (REPLICAS, PAGES_REP, PAGE, RANK + ROPE)
    inner_key = jax.random.fold_in(key, 7002)
    values = jax.random.truncated_normal(inner_key, -4.0, 4.0, full_shape, jnp.float32)
    return values


def draw_cache_codes(key, part):
    values = pool_values(key)
    return values.astype(jnp.bfloat16)


def draw_queries(key, part):
    total_seqs = REPLICAS * SEQ_REP
    full_shape = (total_seqs, Q, H, NOPE + ROPE)
    inner_key = jax.random.fold_in(key, 7003)
    values = jax.random.truncated_normal(inner_key, -4.0, 4.0, full_shape, jnp.float32)
    return values.reshape(REPLICAS, SEQ_REP, Q, H * (NOPE + ROPE)).astype(jnp.bfloat16)


def draw_page_table(key, part):
    return layout(key)[0]


def draw_offsets(key, part):
    return layout(key)[1]


def set_ends(values, key, least, high):
    place = [jax.random.randint(jax.random.fold_in(key, axis), (), 0, length) for axis, length in enumerate(values.shape)]
    longest = values.shape.index(max(values.shape))
    neighbour = place[:longest] + [(place[longest] + 1) % values.shape[longest]] + place[longest + 1:]
    return values.at[tuple(place)].set(least).at[tuple(neighbour)].set(high)


def level_of(rng, extent, cuts, smallest, largest):
    gain, own = 1.0, jax.random.fold_in(rng, 6)
    for axis_at, shards_of in cuts:
        heights = jnp.exp(jax.random.uniform(jax.random.fold_in(own, axis_at), (shards_of,), jnp.float32, smallest / len(cuts), largest / len(cuts)))
        gain = gain * jnp.repeat(heights, extent[axis_at] // shards_of).reshape([-1 if axis == axis_at else 1 for axis in range(len(extent))])
    return gain


def centred(stream_key, shape, scale, limit, cuts=(), kind=jnp.bfloat16):
    entries = scale * jax.random.normal(stream_key, shape, jnp.float32)
    if cuts:
        entries = entries * level_of(stream_key, shape, cuts, -0.22, 0.18)
    return jnp.clip(entries, -limit, limit).astype(kind)


def setup_inputs(seed: int = 0) -> dict:
    splits = jax.random.split(jax.random.key(seed), 9)
    queries = draw_queries(jax.random.fold_in(splits[8], 71), 0)
    grad_out = centred(splits[1], (REPLICAS, SEQ_REP, Q, H * VDIM), 1.0, 6.0, ((0, 2), (1, 16)))
    cache_codes = draw_cache_codes(jax.random.fold_in(splits[8], 71), 0)
    cache_exponents = set_ends(jax.random.randint(splits[3], (REPLICAS, PAGES_REP, PAGE, SCALES), -1, 2), jax.random.fold_in(splits[3], 1), -1, 1).astype(jnp.int32)
    page_table = draw_page_table(jax.random.fold_in(splits[8], 71), 0)
    offsets = draw_offsets(jax.random.fold_in(splits[8], 71), 0)
    key_up = centred(splits[6], (H, RANK, NOPE), RANK ** -0.5, 0.25, ((0, 16),))
    value_up = centred(splits[7], (H, RANK, VDIM), RANK ** -0.5, 0.25, ((0, 16),))
    return dict(queries=queries, grad_out=grad_out, cache_codes=cache_codes, cache_exponents=cache_exponents, page_table=page_table, offsets=offsets, key_up=key_up, value_up=value_up)


def rounded(value):
    return lax.optimization_barrier(value.astype(jnp.bfloat16)).astype(jnp.float32)


def dequantize(stored, exponents):
    block_size = RANK // exponents.shape[-1]
    factor = jnp.repeat(jnp.exp2(exponents.astype(jnp.float32)), block_size, axis=-1)
    latent = (stored[..., :RANK].astype(jnp.float32) * factor).astype(jnp.bfloat16)
    return jnp.concatenate([latent, stored[..., RANK:]], axis=-1)


def sequence_grads(query_rows, grad_rows, seq_keys, start, key_up, value_up):
    head_count = key_up.shape[0]
    row_count = query_rows.shape[0]
    key_count = seq_keys.shape[0]
    softmax_scale = (NOPE + ROPE) ** -0.5
    split_rows = query_rows.reshape(row_count, head_count, NOPE + ROPE).astype(jnp.float32)
    query_nope = split_rows[:, :, :NOPE]
    query_rope = jnp.transpose(split_rows[:, :, NOPE:], (1, 0, 2))
    up_keys = key_up.astype(jnp.float32)
    up_values = value_up.astype(jnp.float32)
    keys_wide = seq_keys.astype(jnp.float32)
    latent = keys_wide[:, :RANK]
    query_lat = rounded(jnp.einsum("qhd,hrd->hqr", query_nope, up_keys))
    query_full = jnp.concatenate([query_lat, query_rope], axis=-1)
    scores = jnp.einsum("hqc,kc->hqk", query_full, keys_wide) * softmax_scale
    position = start + jnp.arange(row_count, dtype=jnp.int32)
    visible = jnp.arange(key_count, dtype=jnp.int32)[None, :] <= position[:, None]
    scores = jnp.where(visible[None], scores, -jnp.inf)
    row_max = jnp.max(scores, axis=-1, keepdims=True)
    exp_scores = jnp.exp(scores - row_max)
    attention = exp_scores / jnp.sum(exp_scores, axis=-1, keepdims=True)
    attention_low = rounded(attention)
    out_latent = jnp.einsum("hqk,kr->hqr", attention_low, latent)
    grad_split = grad_rows.reshape(row_count, head_count, VDIM).astype(jnp.float32)
    grad_latent = jnp.einsum("qhv,hrv->hqr", grad_split, up_values)
    grad_latent_low = rounded(grad_latent)
    row_delta = jnp.sum(grad_latent * out_latent, axis=-1, keepdims=True)
    grad_attention = jnp.einsum("hqr,kr->hqk", grad_latent_low, latent)
    grad_scores = rounded(attention * (grad_attention - row_delta) * softmax_scale)
    grad_full = jnp.einsum("hqk,kc->hqc", grad_scores, keys_wide)
    grad_qlat = rounded(grad_full[..., :RANK])
    grad_nope = jnp.einsum("hqr,hrd->qhd", grad_qlat, up_keys)
    grad_rope = jnp.transpose(grad_full[..., RANK:], (1, 0, 2))
    grad_query = jnp.concatenate([grad_nope, grad_rope], axis=-1)
    grad_query = grad_query.reshape(row_count, head_count * (NOPE + ROPE)).astype(jnp.bfloat16)
    grad_keys = jnp.einsum("hqk,hqc->kc", grad_scores, query_full)
    grad_values = jnp.einsum("hqk,hqr->kr", attention_low, grad_latent_low)
    grad_keys = grad_keys + jnp.pad(grad_values, ((0, 0), (0, ROPE)))
    grad_key_up = jnp.einsum("hqr,qhd->hrd", grad_qlat, query_nope)
    grad_value_up = jnp.einsum("hqr,qhv->hrv", rounded(out_latent), grad_split)
    return grad_query, grad_keys, grad_key_up, grad_value_up


def reference(queries, grad_out, cache_codes, cache_exponents, page_table, offsets, key_up, value_up):
    key_pool = dequantize(cache_codes, cache_exponents)
    total_seqs = REPLICAS * SEQ_REP
    flat_queries = queries.reshape(total_seqs, Q, H * (NOPE + ROPE))
    flat_grads = grad_out.reshape(total_seqs, Q, H * VDIM)
    flat_table = page_table.reshape(total_seqs, CTX // PAGE)
    flat_offsets = offsets.reshape(total_seqs)

    def seq_step(totals, seq_index):
        replica = seq_index // SEQ_REP
        seq_keys = key_pool[replica][flat_table[seq_index]].reshape(CTX, RANK + ROPE)
        results = sequence_grads(flat_queries[seq_index], flat_grads[seq_index], seq_keys, flat_offsets[seq_index], key_up, value_up)
        return (totals[0] + results[2], totals[1] + results[3]), (results[0], results[1])

    zero_sums = (jnp.zeros(key_up.shape, jnp.float32), jnp.zeros(value_up.shape, jnp.float32))
    weight_sums, outputs = lax.scan(seq_step, zero_sums, jnp.arange(total_seqs, dtype=jnp.int32))
    grad_queries = outputs[0].reshape(REPLICAS, SEQ_REP, Q, H * (NOPE + ROPE))
    key_pages = outputs[1].reshape(REPLICAS, PAGES_REP, PAGE, RANK + ROPE)
    replica_ids = jnp.arange(REPLICAS, dtype=jnp.int32)[:, None]
    grad_cache = jnp.zeros(key_pages.shape, jnp.float32).at[replica_ids, page_table.reshape(REPLICAS, PAGES_REP)].set(key_pages)
    return grad_queries, grad_cache, weight_sums[0], weight_sums[1]
```

```python
import functools

import jax
import jax.numpy as jnp
from jax import lax
from jax.experimental import pallas as pl
from jax.experimental.pallas import tpu as pltpu
from jax.sharding import PartitionSpec as P

LANES = 128
NT = (((1,), (1,)), ((), ()))
TN = (((0,), (0,)), ((), ()))


def dequantize(stored, exponents, rank):
    block_size = rank // exponents.shape[-1]
    factor = jnp.repeat(jnp.exp2(exponents.astype(jnp.float32)), block_size, axis=-1)
    latent = (stored[..., :rank].astype(jnp.float32) * factor).astype(jnp.bfloat16)
    return jnp.concatenate([latent, stored[..., rank:]], axis=-1)


def matmul(a, b, dims=None):
    if dims is None:
        return jnp.dot(a, b, preferred_element_type=jnp.float32)
    return lax.dot_general(a, b, dims, preferred_element_type=jnp.float32)


def pair_kernel(
    softmax_scale, offset_ref, q_ref, g_ref, w_ref, lat_ref, lat_t_ref, rope_ref,
    base_lat_ref, base_rope_ref, filled_ref,
    dq_ref, dw_ref, dlat_ref, drope_ref, kv_scratch, grad_scratch,
):
    seqs, rows, width = q_ref.shape
    keys = lat_ref.shape[0] // seqs
    half = LANES // 2

    @pl.when(pl.program_id(0) == 0)
    def _():
        dlat_ref[...] = base_lat_ref[...]
        drope_ref[...] = base_rope_ref[...]

    weights = w_ref[0]
    kv = matmul(lat_ref[...], weights)
    low = lax.broadcasted_iota(jnp.int32, (lat_ref.shape[0], LANES), 1) < half
    rope = rope_ref[...]
    turned = pltpu.roll(kv[:, LANES : 2 * LANES], half, 1)
    kv_scratch[:, :LANES] = kv[:, :LANES].astype(jnp.bfloat16)
    kv_scratch[:, LANES : 2 * LANES] = jnp.where(low, rope, turned).astype(jnp.bfloat16)
    kv_scratch[:, 2 * LANES : width] = jnp.where(low, turned, rope).astype(jnp.bfloat16)
    kv_scratch[:, width:] = kv[:, 2 * LANES :].astype(jnp.bfloat16)

    lane_q = lax.broadcasted_iota(jnp.int32, (rows, width), 1) < width // 2
    key_at = lax.broadcasted_iota(jnp.int32, (keys, 2 * rows), 0)
    lane = lax.broadcasted_iota(jnp.int32, (keys, 2 * rows), 1)
    query_at = jnp.where(lane < rows, lane, lane - rows)
    zero_g = jnp.zeros((rows, LANES), jnp.bfloat16)
    for s in range(seqs):
        span = slice(s * keys, (s + 1) * keys)
        q = q_ref[s]
        zero_q = jnp.zeros_like(q)
        q_two = jnp.concatenate([jnp.where(lane_q, q, zero_q), jnp.where(lane_q, zero_q, q)], axis=0)
        g = g_ref[s]
        g_two = jnp.concatenate(
            [
                jnp.concatenate([g[:, :LANES], zero_g], axis=1),
                jnp.concatenate([zero_g, g[:, LANES:]], axis=1),
            ],
            axis=0,
        )
        k = kv_scratch[span, :width]
        v = kv_scratch[span, width:]
        scores = matmul(k, q_two, NT) * softmax_scale
        visible = key_at <= query_at + offset_ref[s]
        scores = jnp.where(visible, scores, -jnp.inf)
        exp_scores = jnp.exp(scores - jnp.max(scores, axis=0, keepdims=True))
        attention = exp_scores / jnp.sum(exp_scores, axis=0, keepdims=True)
        attention_low = attention.astype(jnp.bfloat16)
        grad_attention = matmul(v, g_two, NT)
        row_delta = jnp.sum(attention_low.astype(jnp.float32) * grad_attention, axis=0, keepdims=True)
        grad_scores = (attention * (grad_attention - row_delta) * softmax_scale).astype(jnp.bfloat16)
        dq = matmul(grad_scores, k, TN)
        dq_ref[s] = jnp.where(lane_q, dq[:rows], dq[rows:]).astype(jnp.bfloat16)
        dk = matmul(grad_scores, q_two)
        dv = matmul(attention_low, g_two)
        low_s = low[:keys]
        first, middle, last = dk[:, :LANES], dk[:, LANES : 2 * LANES], dk[:, 2 * LANES :]
        drope_ref[span, :] += jnp.where(low_s, middle, last)
        second = pltpu.roll(jnp.where(low_s, last, middle), half, 1)
        grad_scratch[span, :LANES] = first.astype(jnp.bfloat16)
        grad_scratch[span, LANES : 2 * LANES] = second.astype(jnp.bfloat16)
        grad_scratch[span, 2 * LANES :] = dv.astype(jnp.bfloat16)
    grads = grad_scratch[...]
    dlat_ref[...] += matmul(grads, weights, NT)
    dw_ref[0] = matmul(lat_t_ref[...], grads).astype(jnp.bfloat16)


def pair_grads(offsets, queries, grads, weights, lat, lat_t, rope2, base_lat, base_rope, filled, chunk, chunks):
    owners, rank, columns = weights.shape
    seqs, rows, _ = queries.shape
    key_rows = lat.shape[0]
    width = queries.shape[2] // (owners * chunks)
    v_width = grads.shape[2] // (owners * chunks)
    softmax_scale = (width // 2) ** (-0.5)
    whole = lambda i, off: (0, 0)
    rows_of = lambda i, off: (0, 0, i * chunks + chunk)
    return pl.pallas_call(
        functools.partial(pair_kernel, softmax_scale),
        grid_spec=pltpu.PrefetchScalarGridSpec(
            num_scalar_prefetch=1,
            grid=(owners,),
            in_specs=[
                pl.BlockSpec((seqs, rows, width), rows_of),
                pl.BlockSpec((seqs, rows, v_width), rows_of),
                pl.BlockSpec((1, rank, columns), lambda i, off: (i, 0, 0)),
                pl.BlockSpec((key_rows, rank), whole),
                pl.BlockSpec((rank, key_rows), whole),
                pl.BlockSpec((key_rows, LANES), whole),
                pl.BlockSpec((key_rows, rank), whole),
                pl.BlockSpec((key_rows, LANES), whole),
                pl.BlockSpec(memory_space=pl.ANY),
            ],
            out_specs=[
                pl.BlockSpec((seqs, rows, width), rows_of),
                pl.BlockSpec((1, rank, columns), lambda i, off: (i, 0, 0)),
                pl.BlockSpec((key_rows, rank), whole),
                pl.BlockSpec((key_rows, LANES), whole),
            ],
            scratch_shapes=[
                pltpu.VMEM((key_rows, width + v_width), jnp.bfloat16),
                pltpu.VMEM((key_rows, columns), jnp.bfloat16),
            ],
        ),
        out_shape=[
            jax.ShapeDtypeStruct(queries.shape, jnp.bfloat16),
            jax.ShapeDtypeStruct(weights.shape, jnp.bfloat16),
            jax.ShapeDtypeStruct((key_rows, rank), jnp.float32),
            jax.ShapeDtypeStruct((key_rows, LANES), jnp.float32),
        ],
        input_output_aliases={9: 0} if chunk else {},
        compiler_params=pltpu.CompilerParams(vmem_limit_bytes=40 * 2**20),
        cost_estimate=pl.CostEstimate(
            flops=owners * 2 * (3 * key_rows * rank * columns + key_rows * 2 * rows * (3 * width + 2 * v_width)),
            bytes_accessed=owners * (2 * seqs * rows * (2 * width + v_width) + 4 * rank * columns),
            transcendentals=owners * key_rows * 2 * rows,
        ),
        name=f"pair_grads_{chunk}",
    )(offsets, queries, grads, weights, lat, lat_t, rope2, base_lat, base_rope, filled)


def local(queries, grad_out, cache_codes, cache_exponents, page_table, offsets, key_up, value_up):
    axes = ("sa", "sb")
    heads, rank, nope = key_up.shape
    _, seqs, rows, _ = queries.shape
    pages, page, full = cache_codes.shape[1:]
    rope_width = full - rank
    me = lax.axis_index(axes)
    chunks = heads // 2

    pool = lax.all_gather(dequantize(cache_codes, cache_exponents, rank)[0], axes, axis=0, tiled=True)
    gathered = []
    for c in range(chunks):
        block = jnp.concatenate(
            [key_up[2 * c], key_up[2 * c + 1], value_up[2 * c], value_up[2 * c + 1]], axis=1
        )
        gathered.append(lax.all_gather(block, axes, axis=0, tiled=False))

    table = page_table[0].reshape(-1)
    own = lax.dynamic_slice_in_dim(table, me * pages, pages)
    inverse = jnp.zeros_like(table).at[table].set(jnp.arange(table.shape[0], dtype=table.dtype))
    own_inverse = lax.dynamic_slice_in_dim(inverse, me * pages, pages)
    my_offsets = lax.dynamic_slice_in_dim(offsets[0], me * seqs, seqs)

    keys = pool[own].reshape(pages * page, full)
    lat = keys[:, :rank]
    lat_t = lat.T
    rope = keys[:, rank:].astype(jnp.float32)
    rope2 = jnp.concatenate([rope, rope], axis=1)
    grad_lat = jnp.zeros((pages * page, rank), jnp.float32)
    grad_rope = jnp.zeros((pages * page, 2 * rope_width), jnp.float32)
    grad_queries = queries[0]
    weight_parts = []
    for c in range(chunks):
        grad_queries, dw, grad_lat, grad_rope = pair_grads(
            my_offsets, queries[0], grad_out[0], gathered[c], lat, lat_t, rope2, grad_lat, grad_rope,
            grad_queries, c, chunks
        )
        mine = lax.psum_scatter(dw, axes, scatter_dimension=0, tiled=True)
        weight_parts.append(lax.psum(mine[0], "rep").astype(jnp.float32))

    grad_keys = jnp.concatenate(
        [grad_lat, grad_rope[:, :rope_width] + grad_rope[:, rope_width:]], axis=1
    ).astype(jnp.bfloat16)
    all_pages = lax.all_gather(grad_keys.reshape(pages, page, full), axes, axis=0, tiled=True)
    grad_cache = all_pages[own_inverse].astype(jnp.float32)[None]
    split = [part.reshape(rank, 4, nope) for part in weight_parts]
    grad_key_up = jnp.stack([part[:, i] for part in split for i in (0, 1)])
    grad_value_up = jnp.stack([part[:, i] for part in split for i in (2, 3)])
    return (grad_queries[None], grad_cache, grad_key_up, grad_value_up)


def solution(mesh):
    in_specs = (
        P("rep", ("sa", "sb"), None, None),
        P("rep", ("sa", "sb"), None, None),
        P("rep", ("sa", "sb"), None, None),
        P("rep", ("sa", "sb"), None, None),
        P("rep", None, None),
        P("rep", None),
        P(("sa", "sb"), None, None),
        P(("sa", "sb"), None, None),
    )
    out_specs = (
        P("rep", ("sa", "sb"), None, None),
        P("rep", ("sa", "sb"), None, None),
        P(("sa", "sb"), None, None),
        P(("sa", "sb"), None, None),
    )
    return jax.shard_map(local, mesh=mesh, in_specs=in_specs, out_specs=out_specs, check_vma=False)
```

```python
import functools

import jax
import jax.numpy as jnp
from jax import lax
from jax.experimental import pallas as pl
from jax.experimental.pallas import tpu as pltpu
from jax.sharding import PartitionSpec as P

LANES = 128
NT = (((1,), (1,)), ((), ()))
TN = (((0,), (0,)), ((), ()))


def dequantize(stored, exponents, rank):
    block_size = rank // exponents.shape[-1]
    factor = jnp.repeat(jnp.exp2(exponents.astype(jnp.float32)), block_size, axis=-1)
    latent = (stored[..., :rank].astype(jnp.float32) * factor).astype(jnp.bfloat16)
    return jnp.concatenate([latent, stored[..., rank:]], axis=-1)


def matmul(a, b, dims=None):
    if dims is None:
        return jnp.dot(a, b, preferred_element_type=jnp.float32)
    return lax.dot_general(a, b, dims, preferred_element_type=jnp.float32)


def pair_kernel(
    softmax_scale, offset_ref, q_ref, g_ref, w_ref, lat_ref, lat_t_ref, rope_ref,
    dq_ref, dw_ref, dlat_ref, drope_ref, kv_scratch, grad_scratch,
):
    seqs, rows, _ = q_ref.shape
    pairs = w_ref.shape[0]
    width = q_ref.shape[2] // pairs
    v_width = g_ref.shape[2] // pairs
    keys = lat_ref.shape[0] // seqs
    half = LANES // 2

    @pl.when(pl.program_id(0) == 0)
    def _():
        dlat_ref[...] = jnp.zeros_like(dlat_ref)
        drope_ref[...] = jnp.zeros_like(drope_ref)

    low = lax.broadcasted_iota(jnp.int32, (lat_ref.shape[0], LANES), 1) < half
    lane_q = lax.broadcasted_iota(jnp.int32, (rows, width), 1) < width // 2
    key_at = lax.broadcasted_iota(jnp.int32, (keys, 2 * rows), 0)
    lane = lax.broadcasted_iota(jnp.int32, (keys, 2 * rows), 1)
    query_at = jnp.where(lane < rows, lane, lane - rows)
    zero_g = jnp.zeros((rows, LANES), jnp.bfloat16)
    zero_q = jnp.zeros((rows, width), jnp.bfloat16)
    low_s = low[:keys]

    def up(p):
        kv = matmul(lat_ref[...], w_ref[p])
        rope = rope_ref[...]
        turned = pltpu.roll(kv[:, LANES : 2 * LANES], half, 1)
        kv_scratch[p, :, :LANES] = kv[:, :LANES].astype(jnp.bfloat16)
        kv_scratch[p, :, LANES : 2 * LANES] = jnp.where(low, rope, turned).astype(jnp.bfloat16)
        kv_scratch[p, :, 2 * LANES : width] = jnp.where(low, turned, rope).astype(jnp.bfloat16)
        kv_scratch[p, :, width:] = kv[:, 2 * LANES :].astype(jnp.bfloat16)

    def attend(p, s):
        span = slice(s * keys, (s + 1) * keys)
        q = q_ref[s, :, p * width : (p + 1) * width]
        q_two = jnp.concatenate([jnp.where(lane_q, q, zero_q), jnp.where(lane_q, zero_q, q)], axis=0)
        g = g_ref[s, :, p * v_width : (p + 1) * v_width]
        g_two = jnp.concatenate(
            [
                jnp.concatenate([g[:, :LANES], zero_g], axis=1),
                jnp.concatenate([zero_g, g[:, LANES:]], axis=1),
            ],
            axis=0,
        )
        k = kv_scratch[p, span, :width]
        v = kv_scratch[p, span, width:]
        scores = matmul(k, q_two, NT) * softmax_scale
        grad_attention = matmul(v, g_two, NT)
        visible = key_at <= query_at + offset_ref[s]
        scores = jnp.where(visible, scores, -jnp.inf)
        exp_scores = jnp.exp(scores - jnp.max(scores, axis=0, keepdims=True))
        attention = exp_scores / jnp.sum(exp_scores, axis=0, keepdims=True)
        attention_low = attention.astype(jnp.bfloat16)
        row_delta = jnp.sum(attention_low.astype(jnp.float32) * grad_attention, axis=0, keepdims=True)
        grad_scores = (attention * (grad_attention - row_delta) * softmax_scale).astype(jnp.bfloat16)
        dq = matmul(grad_scores, k, TN)
        dk = matmul(grad_scores, q_two)
        dv = matmul(attention_low, g_two)
        dq_ref[s, :, p * width : (p + 1) * width] = jnp.where(lane_q, dq[:rows], dq[rows:]).astype(jnp.bfloat16)
        first, middle, last = dk[:, :LANES], dk[:, LANES : 2 * LANES], dk[:, 2 * LANES :]
        drope_ref[span, :] += jnp.where(low_s, middle, last)
        second = pltpu.roll(jnp.where(low_s, last, middle), half, 1)
        grad_scratch[p, span, :LANES] = first.astype(jnp.bfloat16)
        grad_scratch[p, span, LANES : 2 * LANES] = second.astype(jnp.bfloat16)
        grad_scratch[p, span, 2 * LANES :] = dv.astype(jnp.bfloat16)

    def down(p):
        grads = grad_scratch[p]
        dlat_ref[...] += matmul(grads, w_ref[p], NT)
        dw_ref[p] = matmul(lat_t_ref[...], grads).astype(jnp.bfloat16)

    for step in range(pairs + 2):
        if step < pairs:
            up(step)
        if 0 <= step - 1 < pairs:
            for s in range(seqs):
                attend(step - 1, s)
        if step >= 2:
            down(step - 2)


def pair_grads(offsets, queries, grads, weights, lat, lat_t, rope2):
    pairs, rank, columns = weights.shape
    seqs, rows, _ = queries.shape
    key_rows = lat.shape[0]
    block = next(n for n in (4, 2, 1) if pairs % n == 0)
    width = queries.shape[2] // (pairs)
    v_width = grads.shape[2] // (pairs)
    softmax_scale = (width // 2) ** (-0.5)
    whole = lambda i, off: (0, 0)
    rows_of = lambda i, off: (0, 0, i)
    return pl.pallas_call(
        functools.partial(pair_kernel, softmax_scale),
        grid_spec=pltpu.PrefetchScalarGridSpec(
            num_scalar_prefetch=1,
            grid=(pairs // block,),
            in_specs=[
                pl.BlockSpec((seqs, rows, block * width), rows_of),
                pl.BlockSpec((seqs, rows, block * v_width), rows_of),
                pl.BlockSpec((block, rank, columns), lambda i, off: (i, 0, 0)),
                pl.BlockSpec((key_rows, rank), whole),
                pl.BlockSpec((rank, key_rows), whole),
                pl.BlockSpec((key_rows, LANES), whole),
            ],
            out_specs=[
                pl.BlockSpec((seqs, rows, block * width), rows_of),
                pl.BlockSpec((block, rank, columns), lambda i, off: (i, 0, 0)),
                pl.BlockSpec((key_rows, rank), whole),
                pl.BlockSpec((key_rows, LANES), whole),
            ],
            scratch_shapes=[
                pltpu.VMEM((block, key_rows, width + v_width), jnp.bfloat16),
                pltpu.VMEM((block, key_rows, columns), jnp.bfloat16),
            ],
        ),
        out_shape=[
            jax.ShapeDtypeStruct(queries.shape, jnp.bfloat16),
            jax.ShapeDtypeStruct(weights.shape, jnp.bfloat16),
            jax.ShapeDtypeStruct((key_rows, rank), jnp.float32),
            jax.ShapeDtypeStruct((key_rows, LANES), jnp.float32),
        ],
        compiler_params=pltpu.CompilerParams(vmem_limit_bytes=40 * 2**20),
        cost_estimate=pl.CostEstimate(
            flops=pairs * 2 * (3 * key_rows * rank * columns + key_rows * 2 * rows * (3 * width + 2 * v_width)),
            bytes_accessed=pairs * (2 * seqs * rows * (2 * width + v_width) + 4 * rank * columns),
            transcendentals=pairs * key_rows * 2 * rows,
        ),
        name="pair_grads",
    )(offsets, queries, grads, weights, lat, lat_t, rope2)


CORES = 2
MESH = pl.DeviceIdType.MESH


def place():
    column = lax.axis_index("sb")
    return lax.axis_index("sa"), column // CORES, column % CORES, lax.axis_index("rep")


def device(z, x, c, r):
    return {"sa": z, "sb": x * CORES + c, "rep": r}


def gather_kernel(
    depth, columns, reps, w_ref, p_ref, w_out, p_out,
    local_sem, w_send, w_recv, p_send, p_recv,
):
    z, x, c, r = place()
    rows = w_ref.shape[1] // reps

    def owner_of(z_at, x_at, c_at):
        return (z_at * columns + x_at) * CORES + c_at

    me = owner_of(z, x, c)
    other = 1 - c
    barrier = pltpu.get_barrier_semaphore()
    greeted = [
        (z + 1 < depth, (z + 1, x, c, r)),
        (z > 0, (z - 1, x, c, r)),
        (x + 1 < columns, (z, x + 1, c, r)),
        (x > 0, (z, x - 1, c, r)),
        (None, (z, x, other, r)),
    ] + [(None, (z, x, c, lax.rem(r + k, reps))) for k in range(1, reps)]
    for valid, peer in greeted:
        def greet(peer=peer):
            pl.semaphore_signal(barrier, inc=1, device_id=device(*peer), device_id_type=MESH)
        if valid is None:
            greet()
        else:
            pl.when(valid)(greet)
    pl.semaphore_wait(barrier, sum(1 if valid is None else valid.astype(jnp.int32) for valid, _ in greeted))

    def weights_of(ref, part):
        if part is None:
            return ref
        return ref.at[:, pl.ds(part * rows, rows), :]

    def weight_copy(owner, part, kind, peer):
        source = w_ref if owner is me else w_out.at[owner]
        slot = 0 if part is None else part
        return pltpu.make_async_remote_copy(
            src_ref=weights_of(source, part),
            dst_ref=weights_of(w_out.at[owner], part),
            send_sem=w_send.at[kind, owner, slot],
            recv_sem=w_recv.at[owner, slot],
            device_id=device(*peer),
            device_id_type=MESH,
        )

    def page_copy(owner, kind, peer):
        return pltpu.make_async_remote_copy(
            src_ref=p_ref if owner is me else p_out.at[owner],
            dst_ref=p_out.at[owner],
            send_sem=p_send.at[kind, owner],
            recv_sem=p_recv.at[owner],
            device_id=device(*peer),
            device_id_type=MESH,
        )

    def receive_weights(owner, part):
        weight_copy(owner, part, 0, (z, x, other, r)).wait_recv()

    def receive_pages(owner):
        page_copy(owner, 0, (z, x, other, r)).wait_recv()

    def walk(act, receive):
        def send_weights(owner, part, kind, peer):
            act(weight_copy(owner, part, kind, peer))

        def send_pages(owner, kind, peer):
            act(page_copy(owner, kind, peer))

        def along_x(owner, up, down):
            def one_way(kind, to):
                send_weights(owner, r, kind, (z, to, c, r))
                send_pages(owner, kind, (z, to, c, r))
            if up:
                pl.when(x + 1 < columns)(lambda: one_way(2, x + 1))
            if down:
                pl.when(x > 0)(lambda: one_way(3, x - 1))

        def along_z(owner, up, down):
            def one_way(kind, to):
                send_pages(owner, kind, (to, x, c, r))
                send_weights(owner, None, kind, (to, x, c, r))
            if up:
                pl.when(z + 1 < depth)(lambda: one_way(0, z + 1))
            if down:
                pl.when(z > 0)(lambda: one_way(1, z - 1))

        def to_core(owner, part):
            send_weights(owner, part, 4, (z, x, other, r))

        def page_to_core(owner):
            send_pages(owner, 4, (z, x, other, r))

        along_z(me, True, True)
        along_x(me, True, True)
        page_to_core(me)
        to_core(me, None)

        def from_x(x_at, z_at, up):
            owner = owner_of(z_at, x_at, c)
            if receive:
                receive_pages(owner)
                receive_weights(owner, r)
            along_x(owner, up, not up)
            page_to_core(owner)
            for k in range(1, reps):
                send_weights(owner, r, 4 + k, (z, x, c, lax.rem(r + k, reps)))
            to_core(owner, r)

        def rest(x_at, z_at):
            owner = owner_of(z_at, x_at, c)
            for k in range(1, reps):
                part = lax.rem(r + k, reps)
                if receive:
                    receive_weights(owner, part)
                to_core(owner, part)

        def from_z(z_at, up):
            owner = owner_of(z_at, x, c)
            if receive:
                receive_pages(owner)
                receive_weights(owner, None)
            along_z(owner, up, not up)
            along_x(owner, True, True)
            page_to_core(owner)
            to_core(owner, None)

        def at_z(step, visit):
            if step == 0:
                visit(z, None)
                return
            pl.when(z - step >= 0)(lambda: visit(z - step, True))
            pl.when(z + step < depth)(lambda: visit(z + step, False))

        def at_x(visit):
            for far in range(1, columns):
                pl.when(x - far >= 0)(lambda: visit(x - far, True))
                pl.when(x + far < columns)(lambda: visit(x + far, False))

        for step in range(depth):
            if step > 0:
                at_z(step, from_z)
            at_x(lambda x_at, up: at_z(step, lambda z_at, _: from_x(x_at, z_at, up)))
            if step > 0:
                at_x(lambda x_at, up: at_z(step - 1, lambda z_at, _: rest(x_at, z_at)))
        at_x(lambda x_at, up: at_z(depth - 1, lambda z_at, _: rest(x_at, z_at)))

    own_copies = [
        pltpu.make_async_copy(w_ref, w_out.at[me], local_sem.at[0]),
        pltpu.make_async_copy(p_ref, p_out.at[me], local_sem.at[1]),
    ]
    for copy in own_copies:
        copy.start()
    walk(lambda copy: copy.start(), True)

    def from_core(x_at, parts):
        for z_at in range(depth):
            owner = owner_of(z_at, x_at, other)
            receive_pages(owner)
            for part in parts:
                receive_weights(owner, part)

    from_core(x, [None])
    for far in range(1, columns):
        from_core(lax.rem(x + far, columns), list(range(reps)))
    walk(lambda copy: copy.wait_send(), False)
    for copy in own_copies:
        copy.wait()


def gather_all(weights, pages, depth, columns, reps):
    owners = depth * columns * CORES
    anywhere = pl.BlockSpec(memory_space=pl.ANY)
    kinds = 4 + reps
    return pl.pallas_call(
        functools.partial(gather_kernel, depth, columns, reps),
        in_specs=[anywhere] * 2,
        out_specs=[anywhere] * 2,
        out_shape=[
            jax.ShapeDtypeStruct((owners,) + weights.shape, weights.dtype),
            jax.ShapeDtypeStruct((owners,) + pages.shape, pages.dtype),
        ],
        scratch_shapes=[
            pltpu.SemaphoreType.DMA((2,)),
            pltpu.SemaphoreType.DMA((kinds, owners, reps)),
            pltpu.SemaphoreType.DMA((owners, reps)),
            pltpu.SemaphoreType.DMA((kinds, owners)),
            pltpu.SemaphoreType.DMA((owners,)),
        ],
        compiler_params=pltpu.CompilerParams(collective_id=0, has_side_effects=True),
        cost_estimate=pl.CostEstimate(flops=0, bytes_accessed=2 * owners * weights.size * 2, transcendentals=0),
        name="gather_all",
    )(weights, pages)


def reduce_kernel(
    depth, columns, reps, d_ref, out_ref,
    own, core_in, y_low_in, x_high_in, x_low_in, y_high_in, z_in, final,
    load_sem, core_sem, y_low_sem, x_high_sem, x_low_sem, y_high_sem, z_sem, final_sem,
):
    z, x, c, r = place()
    other = 1 - c
    chunks, rank, _ = out_ref.shape
    half = rank // 2
    share = half // reps

    def turn(value, by, size):
        return lax.rem(value + by, size)

    peers = [(z, x, other, r)]
    peers += [(z, turn(x, k, columns), c, r) for k in range(1, columns)]
    peers += [(z, x, c, turn(r, k, reps)) for k in range(1, reps)]
    peers += [(turn(z, k, depth), x, c, r) for k in range(1, depth)]
    barrier = pltpu.get_barrier_semaphore()
    for peer in peers:
        pl.semaphore_signal(barrier, inc=1, device_id=device(*peer), device_id_type=MESH)
    pl.semaphore_wait(barrier, len(peers))

    def send(source, target, sems, at, peer):
        copy = pltpu.make_async_remote_copy(
            src_ref=source,
            dst_ref=target,
            send_sem=sems.at[(0,) + at],
            recv_sem=sems.at[(1,) + at],
            device_id=device(*peer),
            device_id_type=MESH,
        )
        copy.start()
        return copy

    def low(part):
        return pl.ds(pl.multiple_of(part * share, share), share)

    def high(part):
        return pl.ds(pl.multiple_of(half + part * share, share), share)

    groups = 2 if chunks % 2 == 0 else 1
    size = chunks // groups

    def of_group(g):
        return pl.ds(g * size, size)

    def each(g, visit):
        def step(i, carry):
            visit(i // size, g * size + i % size)
            return carry
        lax.fori_loop(0, depth * size, step, 0)

    def total(*terms):
        value = terms[0].astype(jnp.float32)
        for term in terms[1:]:
            value = value + term.astype(jnp.float32)
        return value.astype(jnp.bfloat16)

    order = [turn(x, k, columns) for k in range(1, columns)] + [x]
    loads, crossed = {}, {}
    for g in range(groups):
        for i, x_at in enumerate(order):
            crossed[g, i] = send(
                d_ref.at[:, x_at, other, of_group(g)], core_in.at[x_at, :, of_group(g)], core_sem, (g, i),
                (z, x, other, r),
            )
            loads[g, i] = pltpu.make_async_copy(
                d_ref.at[:, x_at, c, of_group(g)], own.at[x_at, :, of_group(g)], load_sem.at[g, i]
            )
            loads[g, i].start()
    y_low, x_high, x_low, y_high, along_z, last = {}, {}, {}, {}, {}, {}

    def add_cores(g, i):
        x_at = order[i]
        loads[g, i].wait()
        crossed[g, i].wait_recv()

        def add(zi, ci):
            for rows in (slice(0, half), slice(half, rank)):
                own[x_at, zi, ci, rows, :] = total(own[x_at, zi, ci, rows, :], core_in[x_at, zi, ci, rows, :])

        each(g, add)

    def send_first(g, i):
        x_at = order[i]
        if i < columns - 1:
            x_high[g, i] = send(
                own.at[x_at, :, of_group(g), pl.ds(half, half), :], x_high_in.at[i, :, of_group(g)],
                x_high_sem, (g, i), (z, x_at, c, r),
            )
        for k in range(1, reps):
            part = turn(r, k, reps)
            y_low[g, k, i] = send(
                own.at[x_at, :, of_group(g), low(part), :], y_low_in.at[k - 1, i, :, of_group(g)],
                y_low_sem, (g, k - 1, i), (z, x, c, part),
            )

    def wait_first(g):
        for i in range(columns):
            for k in range(1, reps):
                y_low[g, k, i].wait_recv()
        for i in range(columns - 1):
            x_high[g, i].wait_recv()

    def send_second(g):
        for i, x_at in enumerate(order):
            def add_low(zi, ci):
                terms = [own[x_at, zi, ci, low(r), :]] + [y_low_in[k, i, zi, ci] for k in range(reps - 1)]
                own[x_at, zi, ci, low(r), :] = total(*terms)

            each(g, add_low)
            if i < columns - 1:
                x_low[g, i] = send(
                    own.at[x_at, :, of_group(g), low(r), :], x_low_in.at[i, :, of_group(g)],
                    x_low_sem, (g, i), (z, x_at, c, r),
                )

        def add_high(zi, ci):
            terms = [own[x, zi, ci, half:, :]] + [x_high_in[k, zi, ci] for k in range(columns - 1)]
            own[x, zi, ci, half:, :] = total(*terms)

        each(g, add_high)
        for k in range(1, reps):
            part = turn(r, k, reps)
            y_high[g, k] = send(
                own.at[x, :, of_group(g), high(part), :], y_high_in.at[k - 1, :, of_group(g)],
                y_high_sem, (g, k - 1), (z, x, c, part),
            )

    def send_along_z(g):
        for i in range(columns - 1):
            x_low[g, i].wait_recv()

        def add_low(zi, ci):
            terms = [own[x, zi, ci, low(r), :]] + [x_low_in[k, zi, ci] for k in range(columns - 1)]
            own[x, zi, ci, low(r), :] = total(*terms)

        each(g, add_low)
        for k in range(1, reps):
            y_high[g, k].wait_recv()

        def add_high(zi, ci):
            terms = [own[x, zi, ci, high(r), :]] + [y_high_in[k, zi, ci] for k in range(reps - 1)]
            own[x, zi, ci, high(r), :] = total(*terms)

        each(g, add_high)
        for s, rows_of in enumerate((low, high)):
            for k in range(1, depth):
                z_at = turn(z, k, depth)
                along_z[g, s, k] = send(
                    own.at[x, z_at, of_group(g), rows_of(r), :], z_in.at[k - 1, s, of_group(g)],
                    z_sem, (g, k - 1, s), (z_at, x, c, r),
                )

    def send_last(g):
        for s, rows_of in enumerate((low, high)):
            for k in range(1, depth):
                along_z[g, s, k].wait_recv()
            for ci in range(g * size, (g + 1) * size):
                terms = [own[x, z, ci, rows_of(r), :]] + [z_in[k, s, ci] for k in range(depth - 1)]
                final[ci, rows_of(r), :] = total(*terms)
            for k in range(1, reps):
                mine = final.at[of_group(g), rows_of(r), :]
                last[g, s, k] = send(mine, mine, final_sem, (g, k - 1, s), (z, x, c, turn(r, k, reps)))

    for i in range(columns):
        add_cores(0, i)
        send_first(0, i)
    for g in range(1, groups):
        for i in range(columns):
            add_cores(g, i)
    wait_first(0)
    for g in range(1, groups):
        for i in range(columns):
            send_first(g, i)
    send_second(0)
    send_along_z(0)
    for g in range(1, groups):
        wait_first(g)
        send_second(g)
    send_last(0)
    for g in range(1, groups):
        send_along_z(g)
        send_last(g)
    for copy in last.values():
        copy.wait_recv()
    for ci in range(chunks):
        out_ref[ci] = final[ci].astype(jnp.float32)
    for copies in (crossed, y_low, x_high, x_low, y_high, along_z, last):
        for copy in copies.values():
            copy.wait_send()


def reduce_all(partial, depth, columns, reps):
    chunks, rank, width = partial.shape[3:]
    half = rank // 2
    share = half // reps
    dma = pltpu.SemaphoreType.DMA
    kept = lambda *shape: pltpu.VMEM(shape, jnp.bfloat16)
    lone = lambda size: max(size, 1)
    return pl.pallas_call(
        functools.partial(reduce_kernel, depth, columns, reps),
        in_specs=[pl.BlockSpec(memory_space=pl.ANY)],
        out_specs=pl.BlockSpec(memory_space=pltpu.VMEM),
        out_shape=jax.ShapeDtypeStruct((chunks, rank, width), jnp.float32),
        scratch_shapes=[
            kept(columns, depth, chunks, rank, width),
            kept(columns, depth, chunks, rank, width),
            kept(lone(reps - 1), columns, depth, chunks, share, width),
            kept(lone(columns - 1), depth, chunks, half, width),
            kept(lone(columns - 1), depth, chunks, share, width),
            kept(lone(reps - 1), depth, chunks, share, width),
            kept(lone(depth - 1), 2, chunks, share, width),
            kept(chunks, rank, width),
            dma((2, columns)),
            dma((2, 2, columns)),
            dma((2, 2, lone(reps - 1), columns)),
            dma((2, 2, lone(columns - 1))),
            dma((2, 2, lone(columns - 1))),
            dma((2, 2, lone(reps - 1))),
            dma((2, 2, lone(depth - 1), 2)),
            dma((2, 2, lone(reps - 1), 2)),
        ],
        compiler_params=pltpu.CompilerParams(
            collective_id=1, has_side_effects=True, vmem_limit_bytes=48 * 2**20
        ),
        cost_estimate=pl.CostEstimate(flops=partial.size, bytes_accessed=2 * partial.size, transcendentals=0),
        name="reduce_all",
    )(partial)


def local(depth, columns, reps, queries, grad_out, cache_codes, cache_exponents, page_table, offsets, key_up, value_up):
    axes = ("sa", "sb")
    heads, rank, nope = key_up.shape
    _, seqs, rows, _ = queries.shape
    pages, page, full = cache_codes.shape[1:]
    rope_width = full - rank
    me = lax.axis_index(axes)
    chunks = heads // 2

    def side_by_side(heads_of):
        paired = heads_of.reshape(chunks, 2, rank, nope)
        return jnp.swapaxes(paired, 1, 2).reshape(chunks, rank, 2 * nope)

    own_weights = jnp.concatenate([side_by_side(key_up), side_by_side(value_up)], axis=2)
    own_pages = dequantize(cache_codes, cache_exponents, rank)[0].reshape(pages * page, full)
    weights, pool = gather_all(own_weights, own_pages, depth, columns, reps)
    owners = weights.shape[0]
    weights = weights.reshape((owners * chunks,) + weights.shape[2:])
    pool = pool.reshape(owners * pages, page, full)

    table = page_table[0].reshape(-1)
    own = lax.dynamic_slice_in_dim(table, me * pages, pages)
    inverse = jnp.zeros_like(table).at[table].set(jnp.arange(table.shape[0], dtype=table.dtype))
    own_inverse = lax.dynamic_slice_in_dim(inverse, me * pages, pages)
    my_offsets = lax.dynamic_slice_in_dim(offsets[0], me * seqs, seqs)

    keys = pool[own].reshape(pages * page, full)
    lat = keys[:, :rank]
    lat_t = lat.T
    rope = keys[:, rank:].astype(jnp.float32)
    rope2 = jnp.concatenate([rope, rope], axis=1)
    grad_queries, dw, grad_lat, grad_rope = pair_grads(
        my_offsets, queries[0], grad_out[0], weights, lat, lat_t, rope2
    )
    grad_keys = jnp.concatenate(
        [grad_lat, grad_rope[:, :rope_width] + grad_rope[:, rope_width:]], axis=1
    ).astype(jnp.bfloat16)
    all_pages = lax.all_gather(grad_keys.reshape(pages, page, full), axes, axis=0, tiled=True)
    grad_cache = all_pages[own_inverse].astype(jnp.float32)[None]
    mine = reduce_all(dw.reshape((depth, columns, CORES, chunks) + dw.shape[1:]), depth, columns, reps)
    split = mine.reshape(chunks, rank, 4, nope)
    grad_key_up = jnp.swapaxes(split[:, :, :2], 1, 2).reshape(heads, rank, nope)
    grad_value_up = jnp.swapaxes(split[:, :, 2:], 1, 2).reshape(heads, rank, nope)
    return (grad_queries[None], grad_cache, grad_key_up, grad_value_up)


def solution(mesh):
    in_specs = (
        P("rep", ("sa", "sb"), None, None),
        P("rep", ("sa", "sb"), None, None),
        P("rep", ("sa", "sb"), None, None),
        P("rep", ("sa", "sb"), None, None),
        P("rep", None, None),
        P("rep", None),
        P(("sa", "sb"), None, None),
        P(("sa", "sb"), None, None),
    )
    out_specs = (
        P("rep", ("sa", "sb"), None, None),
        P("rep", ("sa", "sb"), None, None),
        P(("sa", "sb"), None, None),
        P(("sa", "sb"), None, None),
    )
    sizes = (mesh.shape["sa"], mesh.shape["sb"] // CORES, mesh.shape["rep"])
    return jax.shard_map(functools.partial(local, *sizes), mesh=mesh, in_specs=in_specs, out_specs=out_specs, check_vma=False)
```
